512 devices in a mesh: ctx: 128 (over z, y_lo, x), head: 4 (over y_hi, core).
Axes of the slice: x: 4, y: 8 (y_hi: 2, y_lo: 4; y = y_hi * 4 + y_lo), z: 8, core: 2. Of those that a mesh axis runs over, the one named last changes fastest.
Arguments:
- queries: bfloat16 [65536, 1024], P('ctx', 'head'), may hold values from -6 to 6
- key_rows: bfloat16 [65536, 1024], P('ctx', 'head'), may hold values from -6 to 6
- value_rows: bfloat16 [65536, 1024], P('ctx', 'head'), may hold values from -6 to 6
- gating: bfloat16 [65536, 1024], P('ctx', 'head'), may hold values from -6 to 6
- gain_vector: bfloat16 [1024], P('head'), may hold values from 0.099609375 to 1.8984375
- out_grad: bfloat16 [65536, 1024], P('ctx', 'head'), may hold values from -6 to 6
- user_lengths: int32 [4], replicated, may hold values from 1 to 32768, 65536 in all
- cand_counts: int32 [4], replicated, may hold values from 1 to 256
Outputs:
- output: bfloat16 [65536, 1024], P('ctx', 'head')
- query_grad: bfloat16 [65536, 1024], P('ctx', 'head')
- key_grad: bfloat16 [65536, 1024], P('ctx', 'head')
- value_grad: bfloat16 [65536, 1024], P('ctx', 'head')
- gate_grad: bfloat16 [65536, 1024], P('ctx', 'head')
The draws below stay inside these ranges and needn't reach their ends.
Inputs may be any that keep to these rules, and one draw needn't show every extreme that they name: user_lengths sum to 65536; the longest user has exactly 32768 tokens. `cand_counts`: a user's last min(count, length) tokens are its candidates.
All inputs are finite; a program needn't handle non-finite values.
Results may differ from the reference program's by a relative error of at most 0.0052.
The reference program's roundings to bfloat16 on the way (of `attn`, `dmixed` and `dscore`) count: a program that leaves them out, or rounds other values in their place, can miss the bound.
Values may be sent and summed in bfloat16 or wider, within the bound.
A program may use at most 64 MiB of HBM per device.

```python
import math
import jax
import jax.numpy as jnp
import numpy as np
from jax import lax

HD = 128
HEADS = 8
D = 1024
TOK_DEV = 512
BACK = 3
NCAND = 256
USERS = 4
WINDOW = 1536
TOKENS = 65536
LONGEST = 32768


def touch_ends(array, own_key, smallest, high):
    longest = array.shape.index(max(array.shape))
    spots = []
    for shift in (0, 1):
        where = [jax.random.randint(jax.random.fold_in(own_key, axis), (), 0, length) for axis, length in enumerate(array.shape)]
        where[longest] = (where[longest] + shift) % array.shape[longest]
        spots.append(tuple(where))
    return array.at[spots[0]].set(smallest).at[spots[1]].set(high)


def steps_of(key, dims, split, smallest, top_value):
    factor_of = 1.0
    for position, parts in split:
        steps = jax.random.uniform(jax.random.fold_in(jax.random.fold_in(key, 6), position), (parts,), jnp.float32, smallest / len(split), top_value / len(split))
        factor_of = factor_of * jnp.repeat(jnp.exp(steps), dims[position] // parts).reshape((-1,) + (1,) * (len(dims) - 1 - position))
    return factor_of


def split_up(count, total, most, slope):
    portions = [(1 << 20) // math.isqrt(standing ** slope) + 1 for standing in range(2, count + 1)]
    rest, counts = total - most - (count - 1), [1] * (count - 1)
    while rest > 0:
        movable = [i for i in range(count - 1) if counts[i] < most]
        whole, left = sum([portions[i] for i in movable]), rest
        for i in movable:
            more = min(most - counts[i], max(1, left * portions[i] // whole), rest)
            counts[i] = counts[i] + more
            rest = rest - more
    return np.array([most] + counts)


def ragged_sizes(key, count, total, limit, lean):
    if count == 2:
        one = jax.random.randint(key, (), max(1, total - limit), min(limit, total - 1) + 1)
        return jnp.stack([one, total - one])
    sizes = jnp.asarray(split_up(count, total, limit, lean), jnp.int32)
    twos = (count - 1) // 2
    source_of, sink = sizes[1:1 + 2 * twos:2], sizes[2:2 + 2 * twos:2]
    room = jnp.minimum(source_of - 1, limit - sink)
    passed = jax.random.randint(jax.random.fold_in(key, 1), (twos,), 0, 1 << 20) % (room + 1)
    sizes = sizes.at[1:1 + 2 * twos:2].set(source_of - passed).at[2:2 + 2 * twos:2].set(sink + passed)
    return sizes[jax.random.permutation(jax.random.fold_in(key, 2), count)]


def centred(stream_key, extent, deviation, reach, shards=(), kind=jnp.bfloat16):
    result = deviation * jax.random.normal(stream_key, extent, jnp.float32)
    if shards:
        result = result * steps_of(stream_key, extent, shards, -0.22, 0.18)
    return jnp.clip(result, -reach, reach).astype(kind)


def setup_inputs(seed: int = 0) -> dict:
    streams_of = jax.random.split(jax.random.key(seed), 9)
    return {
        "queries": centred(streams_of[0], (TOKENS, D), 1.0, 6.0, ((0, 128), (1, 4))),
        "key_rows": centred(streams_of[1], (TOKENS, D), 1.0, 6.0, ((0, 128), (1, 4))),
        "value_rows": centred(streams_of[2], (TOKENS, D), 1.0, 6.0, ((0, 128), (1, 4))),
        "gating": centred(streams_of[3], (TOKENS, D), 1.0, 6.0, ((0, 128), (1, 4))),
        "gain_vector": jnp.clip(1.0 + 0.18 * jax.random.normal(streams_of[4], (D,), jnp.float32), 0.099609375, 1.8984375).astype(jnp.bfloat16),
        "out_grad": centred(streams_of[5], (TOKENS, D), 1.0, 6.0, ((0, 128), (1, 4))),
        "user_lengths": ragged_sizes(streams_of[6], USERS, TOKENS, LONGEST, 2).astype(jnp.int32),
        "cand_counts": touch_ends(jax.random.randint(streams_of[7], (USERS,), 1, NCAND + 1), jax.random.fold_in(streams_of[7], 1), 1, NCAND).astype(jnp.int32),
    }


norm_eps = 1e-06

def user_bounds(positions, user_lengths, cand_counts):
    ends_at = jnp.cumsum(user_lengths).astype(jnp.int32)
    starts_at = (ends_at - user_lengths).astype(jnp.int32)
    first_cand = (ends_at - jnp.minimum(cand_counts, user_lengths)).astype(jnp.int32)
    inside = (positions[:, None] >= starts_at[None, :]) & (positions[:, None] < ends_at[None, :])
    seg_start = lax.optimization_barrier(jnp.sum(jnp.where(inside, starts_at[None, :], 0), axis=1)).astype(jnp.int32)
    cand_start = lax.optimization_barrier(jnp.sum(jnp.where(inside, first_cand[None, :], 0), axis=1)).astype(jnp.int32)
    return (seg_start, cand_start)

def visible(query_pos, key_pos, seg_start, cand_start):
    before = key_pos[None, :] <= query_pos[:, None]
    recent = query_pos[:, None] - key_pos[None, :] < WINDOW
    same_user = key_pos[None, :] >= seg_start[:, None]
    history = (key_pos[None, :] < cand_start[:, None]) | (key_pos[None, :] == query_pos[:, None])
    return before & recent & same_user & history

def silu_slope(scores):
    sigma = jax.nn.sigmoid(scores)
    return sigma * (1.0 + scores * (1.0 - sigma))

def to_bf16(values):
    return lax.optimization_barrier(values.astype(jnp.bfloat16)).astype(jnp.float32)

def reference(queries, key_rows, value_rows, gating, gain_vector, out_grad, user_lengths, cand_counts):
    scale = 1.0 / math.sqrt(HD)
    positions = jnp.arange(TOKENS, dtype=jnp.int32)
    seg_start, cand_start = user_bounds(positions, user_lengths, cand_counts)
    margin = BACK * TOK_DEV
    width = (BACK + 1) * TOK_DEV
    pad_zero = jnp.zeros((margin, D), jnp.bfloat16)
    keys_pad = jnp.concatenate([pad_zero, key_rows], axis=0).reshape(TOKENS + margin, HEADS, HD)
    values_pad = jnp.concatenate([pad_zero, value_rows], axis=0).reshape(TOKENS + margin, HEADS, HD)
    query_all = queries.reshape(TOKENS, HEADS, HD)
    gain_f = gain_vector.astype(jnp.float32)

    def one_block(carry, block):
        dk_acc, dv_acc = carry
        start = (block * TOK_DEV).astype(jnp.int32)
        query_block = lax.dynamic_slice_in_dim(query_all, start, TOK_DEV, 0).astype(jnp.float32)
        keys_win = lax.dynamic_slice_in_dim(keys_pad, start, width, 0).astype(jnp.float32)
        values_win = lax.dynamic_slice_in_dim(values_pad, start, width, 0).astype(jnp.float32)
        query_pos = start + jnp.arange(TOK_DEV, dtype=jnp.int32)
        key_pos = start - margin + jnp.arange(width, dtype=jnp.int32)
        seg_block = lax.dynamic_slice_in_dim(seg_start, start, TOK_DEV, 0)
        cand_block = lax.dynamic_slice_in_dim(cand_start, start, TOK_DEV, 0)
        allowed = visible(query_pos, key_pos, seg_block, cand_block).astype(jnp.float32)[None]
        scores = jnp.einsum('qhd,khd->hqk', query_block, keys_win) * scale
        attn = to_bf16(jax.nn.silu(scores) * allowed / WINDOW)
        mixed = jnp.einsum('hqk,khd->qhd', attn, values_win).reshape(TOK_DEV, D)
        row_mean = lax.optimization_barrier(jnp.sum(mixed, axis=1)) / D
        row_var = lax.optimization_barrier(jnp.sum(mixed * mixed, axis=1)) / D - row_mean * row_mean
        rstd = lax.rsqrt(row_var + norm_eps)
        normed = (mixed - row_mean[:, None]) * rstd[:, None]
        gate_block = lax.dynamic_slice_in_dim(gating, start, TOK_DEV, 0).astype(jnp.float32)
        grad_block = lax.dynamic_slice_in_dim(out_grad, start, TOK_DEV, 0).astype(jnp.float32)
        output = (normed * gain_f * gate_block).astype(jnp.bfloat16)
        gate_grad = (grad_block * normed * gain_f).astype(jnp.bfloat16)
        dnorm = grad_block * gate_block * gain_f
        mean_one = lax.optimization_barrier(jnp.sum(dnorm, axis=1)) / D
        mean_two = lax.optimization_barrier(jnp.sum(dnorm * normed, axis=1)) / D
        dmixed = to_bf16(rstd[:, None] * (dnorm - mean_one[:, None] - normed * mean_two[:, None]))
        dmixed_heads = dmixed.reshape(TOK_DEV, HEADS, HD)
        dattn = jnp.einsum('qhd,khd->hqk', dmixed_heads, values_win)
        dv_win = jnp.einsum('hqk,qhd->khd', attn, dmixed_heads).reshape(width, D)
        dscore = to_bf16(dattn * silu_slope(scores) * allowed / WINDOW)
        dq_block = (jnp.einsum('hqk,khd->qhd', dscore, keys_win) * scale).reshape(TOK_DEV, D).astype(jnp.bfloat16)
        dk_win = (jnp.einsum('hqk,qhd->khd', dscore, query_block) * scale).reshape(width, D)
        dk_acc = lax.dynamic_update_slice_in_dim(dk_acc, lax.dynamic_slice_in_dim(dk_acc, start, width, 0) + dk_win, start, 0)
        dv_acc = lax.dynamic_update_slice_in_dim(dv_acc, lax.dynamic_slice_in_dim(dv_acc, start, width, 0) + dv_win, start, 0)
        return ((dk_acc, dv_acc), (output, dq_block, gate_grad))
    zero_acc = jnp.zeros((TOKENS + margin, D), jnp.float32)
    blocks = jnp.arange(TOKENS // TOK_DEV, dtype=jnp.int32)
    (dk_acc, dv_acc), (outputs, dq_blocks, gate_blocks) = lax.scan(one_block, (zero_acc, zero_acc), blocks)
    output = outputs.reshape(TOKENS, D)
    query_grad = dq_blocks.reshape(TOKENS, D)
    gate_grad = gate_blocks.reshape(TOKENS, D)
    key_grad = dk_acc[margin:].astype(jnp.bfloat16)
    value_grad = dv_acc[margin:].astype(jnp.bfloat16)
    return (output, query_grad, key_grad, value_grad, gate_grad)
```

```python
import functools
import math

import jax
import jax.numpy as jnp
from jax import lax
from jax.experimental import pallas as pl
from jax.experimental.pallas import tpu as pltpu
from jax.sharding import PartitionSpec as P

HD = 128
D = 1024
T = 512
HALF = 256
BACK = 3
WINDOW = 1536
USERS = 4
NC = 4
CH = T // NC
EPS = 1e-06
SCALE = 1.0 / math.sqrt(HD)
MESH = pl.DeviceIdType.MESH
NT = (((1,), (1,)), ((), ()))
NN = (((1,), (0,)), ((), ()))
TN = (((0,), (0,)), ((), ()))
F32 = jnp.float32
BF16 = jnp.bfloat16


def dot(a, b, dims):
    return lax.dot_general(a, b, dims, preferred_element_type=F32)


def dot_exact(a, b, dims):
    return lax.dot_general(a, b, dims, preferred_element_type=F32, precision=lax.Precision.HIGHEST)


def query_bounds(pos, lengths, cands):
    seg = jnp.zeros_like(pos)
    cand = jnp.zeros_like(pos)
    start = jnp.int32(0)
    for u in range(USERS):
        length = lengths[u]
        end = start + length
        first = end - jnp.minimum(cands[u], length)
        inside = (pos >= start) & (pos < end)
        seg = jnp.where(inside, start, seg)
        cand = jnp.where(inside, first, cand)
        start = end
    return jnp.maximum(seg, pos - (WINDOW - 1)), jnp.minimum(cand, pos)


def weights(prod, allowed):
    h = prod * (0.5 * SCALE)
    w = 1.0 + jnp.tanh(h)
    a = jnp.where(allowed, w * (1.0 / WINDOW), 0.0)
    attn = (h * a).astype(BF16)
    slope = a * (0.5 + h * (1.0 - 0.5 * w))
    return attn, slope


def spans_q(d):
    if d == 0:
        return ((0, 0, HALF), (1, 0, T))
    if d == BACK:
        return ((0, 0, T), (1, HALF, HALF))
    return ((0, 0, T), (1, 0, T))


def spans_k(d):
    if d == 0:
        return ((0, 0, T), (1, HALF, HALF))
    if d == BACK:
        return ((0, 0, HALF), (1, 0, T))
    return ((0, 0, T), (1, 0, T))


def kernel(
    len_ref, cand_ref, gain_ref, q_hbm, k_hbm, v_hbm, gate_hbm, og_hbm,
    out_ref, dq_ref, dk_ref, dv_ref, dgate_ref,
    kbuf, vbuf, qbuf, dbuf, pk, pv, pq, pd, gate, og, mixed, dkacc, dvacc,
    slope_q, attn_k, slope_k, lo_q, hi_q, lo_k, hi_k, stats,
    loc, kvy_s, kvy_r, kvx_s, kvx_r, qy_s, qy_r, qx_s, qx_r, dy_s, dy_r, dx_s, dx_r, st_s, st_r,
):
    c = lax.axis_index("ctx")
    hd = lax.axis_index("head")
    x = lax.rem(c, 4)
    row0 = c - x
    nctx = 128

    def row_peer(d):
        return {"ctx": row0 + lax.rem(x + d + 4, 4), "head": hd}

    def ctx_peer(d):
        return {"ctx": lax.rem(c + d + nctx, nctx), "head": hd}

    def head_peer(e):
        return {"ctx": c, "head": lax.rem(hd + e, 4)}

    bar = pltpu.get_barrier_semaphore()
    peers = [row_peer(1), row_peer(2), row_peer(3), ctx_peer(4), ctx_peer(-4)]
    peers += [head_peer(1), head_peer(2), head_peer(3)]
    for p in peers:
        pl.semaphore_signal(bar, inc=1, device_id=p, device_id_type=MESH)

    loads = [
        pltpu.make_async_copy(src, dst, loc.at[i])
        for i, (src, dst) in enumerate(
            ((q_hbm, qbuf.at[0]), (k_hbm, kbuf.at[0]), (v_hbm, vbuf.at[0]), (gate_hbm, gate), (og_hbm, og))
        )
    ]
    for cp in loads:
        cp.start()
    pl.semaphore_wait(bar, len(peers))

    def rows(ch):
        return pl.ds(ch * CH, CH)

    def remote(src, dst, ss, rs, dev):
        return pltpu.make_async_remote_copy(src, dst, ss, rs, device_id=dev, device_id_type=MESH)

    def kv_y(a, ch):
        src, dst = ((k_hbm, pk), (v_hbm, pv))[a]
        return remote(src.at[rows(ch)], dst.at[rows(ch)], kvy_s.at[a, ch], kvy_r.at[a, ch], ctx_peer(4))

    def kv_x(a, d, ch, own):
        src = ((k_hbm, v_hbm) if own else (pk, pv))[a]
        dst = (kbuf, vbuf)[a]
        return remote(
            src.at[rows(ch)], dst.at[d, rows(ch)], kvx_s.at[a, d - 1, ch], kvx_r.at[a, d - 1, ch], row_peer(d)
        )

    def q_y(ch):
        return remote(q_hbm.at[rows(ch)], pq.at[rows(ch)], qy_s.at[ch], qy_r.at[ch], ctx_peer(-4))

    def q_x(d, ch, own):
        src = q_hbm if own else pq
        return remote(src.at[rows(ch)], qbuf.at[d, rows(ch)], qx_s.at[d - 1, ch], qx_r.at[d - 1, ch], row_peer(-d))

    def d_y(ch):
        return remote(dbuf.at[0, rows(ch)], pd.at[rows(ch)], dy_s.at[ch], dy_r.at[ch], ctx_peer(-4))

    def d_x(d, ch, own):
        src = dbuf.at[0, rows(ch)] if own else pd.at[rows(ch)]
        return remote(src, dbuf.at[d, rows(ch)], dx_s.at[d - 1, ch], dx_r.at[d - 1, ch], row_peer(-d))

    def st(e):
        return remote(stats.at[0], stats.at[e], st_s.at[e - 1], st_r.at[e - 1], head_peer(e))

    @pl.when(x >= 1)
    def _():
        for ch in range(NC):
            for a in range(2):
                kv_y(a, ch).start()

    for d in range(1, BACK + 1):

        @pl.when(x + d < 4)
        def _():
            for ch in range(NC):
                for a in range(2):
                    kv_x(a, d, ch, True).start()

    def fill_rows(t, _):
        r = pl.ds(pl.multiple_of(t * HALF, HALF), HALF)
        pos = c * T + t * HALF + lax.broadcasted_iota(jnp.int32, (HALF, HD), 0)
        lo_q[r, :], hi_q[r, :] = query_bounds(pos, len_ref, cand_ref)
        return 0

    lax.fori_loop(0, 2, fill_rows, 0)
    for d in range(BACK + 1):
        pos = (c + d) * T + lax.broadcasted_iota(jnp.int32, (8, T), 1)
        lo_k[d], hi_k[d] = query_bounds(pos, len_ref, cand_ref)

    mixed[...] = jnp.zeros_like(mixed)
    dkacc[...] = jnp.zeros_like(dkacc)
    dvacc[...] = jnp.zeros_like(dvacc)
    for cp in loads:
        cp.wait()

    def cols(h):
        return pl.ds(pl.multiple_of(h * HD, HD), HD)

    def forward(d):
        def body(h, _):
            hs = cols(h)
            for t, k0, kn in spans_q(d):
                r = pl.ds(t * HALF, HALF)
                prod = dot(qbuf[0, r, hs], kbuf[d, pl.ds(k0, kn), hs], NT)
                key = (c - d) * T + k0 + lax.broadcasted_iota(jnp.int32, (HALF, kn), 1)
                lo = jnp.concatenate([lo_q[r, :]] * (kn // HD), axis=1)
                hi = jnp.concatenate([hi_q[r, :]] * (kn // HD), axis=1)
                allowed = (key >= lo) & (key < hi)
                if d == 0:
                    allowed = allowed | (key == c * T + t * HALF + lax.broadcasted_iota(jnp.int32, (HALF, kn), 0))
                attn, slope = weights(prod, allowed)
                slope_q[h, r, pl.ds(d * T + k0, kn)] = slope
                mixed[r, hs] += dot(attn, vbuf[d, pl.ds(k0, kn), hs], NN)
            return 0

        lax.fori_loop(0, 2, body, 0)

    def keys_before(d):
        def body(h, _):
            hs = cols(h)
            for t, q0, qn in spans_k(d):
                r = pl.ds(t * HALF, HALF)
                prod = dot(kbuf[0, r, hs], qbuf[d, pl.ds(q0, qn), hs], NT)
                key = c * T + t * HALF + lax.broadcasted_iota(jnp.int32, (HALF, qn), 0)
                allowed = (key >= lo_k[d, 0:1, pl.ds(q0, qn)]) & (key < hi_k[d, 0:1, pl.ds(q0, qn)])
                if d == 0:
                    allowed = allowed | (key == c * T + q0 + lax.broadcasted_iota(jnp.int32, (HALF, qn), 1))
                attn, slope = weights(prod, allowed)
                attn_k[h, r, pl.ds(d * T + q0, qn)] = attn
                slope_k[h, r, pl.ds(d * T + q0, qn)] = slope
            return 0

        lax.fori_loop(0, 2, body, 0)

    def keys_after(d):
        def body(h, _):
            hs = cols(h)
            for t, q0, qn in spans_k(d):
                r = pl.ds(t * HALF, HALF)
                dm = dbuf[d, pl.ds(q0, qn), hs]
                dvacc[r, hs] += dot(attn_k[h, r, pl.ds(d * T + q0, qn)], dm, NN)
                dattn = dot(vbuf[0, r, hs], dm, NT)
                dscore = (dattn * slope_k[h, r, pl.ds(d * T + q0, qn)]).astype(BF16)
                dkacc[r, hs] += dot(dscore, qbuf[d, pl.ds(q0, qn), hs], NN)
            return 0

        lax.fori_loop(0, 2, body, 0)

    def query_grad(h, _):
        hs = cols(h)
        for t in range(2):
            r = pl.ds(t * HALF, HALF)
            dm = dbuf[0, r, hs]
            total = jnp.zeros((HALF, HD), F32)
            for d in range(BACK + 1):
                _, k0, kn = spans_q(d)[t]
                dattn = dot(dm, vbuf[d, pl.ds(k0, kn), hs], NT)
                dscore = (dattn * slope_q[h, r, pl.ds(d * T + k0, kn)]).astype(BF16)
                total += dot(dscore, kbuf[d, pl.ds(k0, kn), hs], NN)
            dq_ref[r, hs] = (total * SCALE).astype(BF16)
        return 0

    forward(0)

    @pl.when(x >= 1)
    def _():
        for ch in range(NC):
            for a in range(2):
                kv_y(a, ch).wait_recv()
                for d in range(1, BACK + 1):

                    @pl.when(x + d >= 4)
                    def _():
                        kv_x(a, d, ch, False).start()

    def wait_kv(d):
        for ch in range(NC):
            for a in range(2):
                kv_x(a, d, ch, True).wait_recv()

    wait_kv(1)
    forward(1)

    @pl.when(x <= 2)
    def _():
        for ch in range(NC):
            q_y(ch).start()

    wait_kv(2)
    forward(2)
    wait_kv(3)
    for d in range(1, BACK + 1):

        @pl.when(x - d >= 0)
        def _():
            for ch in range(NC):
                q_x(d, ch, True).start()

    forward(3)

    gain = gain_ref[...].astype(F32)
    pick = lax.broadcasted_iota(jnp.int32, (8, HD), 0)

    def fold(a):
        return a[:, :HD] + a[:, HD:]

    m = mixed[...]
    dnorm = og[...].astype(F32) * gate[...].astype(F32) * gain
    total = jnp.zeros((8, T), F32)
    for i, a in enumerate((m, m * m, dnorm, dnorm * m)):
        total += dot_exact((pick == i).astype(F32), fold(a), NT)
    stats[0] = total
    for e in range(1, 4):
        st(e).start()

    @pl.when(x <= 2)
    def _():
        for ch in range(NC):
            q_y(ch).wait_recv()
            for d in range(1, BACK + 1):

                @pl.when(x - d < 0)
                def _():
                    q_x(d, ch, False).start()

    keys_before(0)
    for e in range(1, 4):
        st(e).wait_recv()
    total = stats[0] + stats[1] + stats[2] + stats[3]
    mean = total[0:1] / D
    var = total[1:2] / D - mean * mean
    rstd = lax.rsqrt(var + EPS)
    mean_one = total[2:3] / D
    mean_two = rstd * (total[3:4] - mean * total[2:3]) / D
    coef = jnp.concatenate([mean, rstd, mean_one, mean_two, jnp.zeros((4, T), F32)], axis=0)
    wide = []
    for i in range(4):
        b = dot_exact(coef, (pick == i).astype(F32), TN)
        wide.append(jnp.concatenate([b, b], axis=1))
    mean, rstd, mean_one, mean_two = wide
    normed = (mixed[...] - mean) * rstd
    gf = gate[...].astype(F32)
    of = og[...].astype(F32)
    dbuf[0] = (rstd * (of * gf * gain - mean_one - normed * mean_two)).astype(BF16)

    @pl.when(x <= 2)
    def _():
        for ch in range(NC):
            d_y(ch).start()

    for d in range(1, BACK + 1):

        @pl.when(x - d >= 0)
        def _():
            for ch in range(NC):
                d_x(d, ch, True).start()

    out_ref[...] = (normed * gain * gf).astype(BF16)
    dgate_ref[...] = (of * normed * gain).astype(BF16)

    query_grad(0, 0)

    @pl.when(x <= 2)
    def _():
        for ch in range(NC):
            d_y(ch).wait_recv()
            for d in range(1, BACK + 1):

                @pl.when(x - d < 0)
                def _():
                    d_x(d, ch, False).start()

    query_grad(1, 0)
    keys_after(0)
    for d in range(1, BACK + 1):
        for ch in range(NC):
            q_x(d, ch, True).wait_recv()
        keys_before(d)
    for d in range(1, BACK + 1):
        for ch in range(NC):
            d_x(d, ch, True).wait_recv()
        keys_after(d)
    dk_ref[...] = (dkacc[...] * SCALE).astype(BF16)
    dv_ref[...] = dvacc[...].astype(BF16)

    @pl.when(x >= 1)
    def _():
        for ch in range(NC):
            for a in range(2):
                kv_y(a, ch).wait_send()

    @pl.when(x <= 2)
    def _():
        for ch in range(NC):
            q_y(ch).wait_send()
            d_y(ch).wait_send()

    for d in range(1, BACK + 1):
        st(d).wait_send()
        for ch in range(NC):
            for a in range(2):
                kv_x(a, d, ch, True).wait_send()
            q_x(d, ch, True).wait_send()
            d_x(d, ch, True).wait_send()


def per_device(queries, key_rows, value_rows, gating, gain_vector, out_grad, user_lengths, cand_counts):
    feat = queries.shape[1]
    block = jax.ShapeDtypeStruct((T, feat), BF16)
    vmem = pl.BlockSpec(memory_space=pltpu.VMEM)
    smem = pl.BlockSpec(memory_space=pltpu.SMEM)
    hbm = pl.BlockSpec(memory_space=pl.ANY)
    sem = pltpu.SemaphoreType.DMA
    output, query_grad, key_grad, value_grad, gate_grad = pl.pallas_call(
        kernel,
        out_shape=[block] * 5,
        in_specs=[smem, smem, vmem, hbm, hbm, hbm, hbm, hbm],
        out_specs=[vmem] * 5,
        scratch_shapes=[
            pltpu.VMEM((4, T, feat), BF16),
            pltpu.VMEM((4, T, feat), BF16),
            pltpu.VMEM((4, T, feat), BF16),
            pltpu.VMEM((4, T, feat), BF16),
            pltpu.VMEM((T, feat), BF16),
            pltpu.VMEM((T, feat), BF16),
            pltpu.VMEM((T, feat), BF16),
            pltpu.VMEM((T, feat), BF16),
            pltpu.VMEM((T, feat), BF16),
            pltpu.VMEM((T, feat), BF16),
            pltpu.VMEM((T, feat), F32),
            pltpu.VMEM((T, feat), F32),
            pltpu.VMEM((T, feat), F32),
            pltpu.VMEM((2, T, 4 * T), F32),
            pltpu.VMEM((2, T, 4 * T), BF16),
            pltpu.VMEM((2, T, 4 * T), F32),
            pltpu.VMEM((T, HD), jnp.int32),
            pltpu.VMEM((T, HD), jnp.int32),
            pltpu.VMEM((4, 8, T), jnp.int32),
            pltpu.VMEM((4, 8, T), jnp.int32),
            pltpu.VMEM((4, 8, T), F32),
            sem((5,)),
            sem((2, NC)), sem((2, NC)), sem((2, BACK, NC)), sem((2, BACK, NC)),
            sem((NC,)), sem((NC,)), sem((BACK, NC)), sem((BACK, NC)),
            sem((NC,)), sem((NC,)), sem((BACK, NC)), sem((BACK, NC)),
            sem((3,)), sem((3,)),
        ],
        compiler_params=pltpu.CompilerParams(
            collective_id=0, has_side_effects=True, vmem_limit_bytes=50 << 20
        ),
        name="hstu",
    )(user_lengths, cand_counts, gain_vector.reshape(1, feat), queries, key_rows, value_rows, gating, out_grad)
    return output, query_grad, key_grad, value_grad, gate_grad


def solution(mesh):
    tokens = P("ctx", "head")
    return jax.shard_map(
        per_device,
        mesh=mesh,
        in_specs=(tokens, tokens, tokens, tokens, P("head"), tokens, P(), P()),
        out_specs=(tokens,) * 5,
        check_vma=False,
    )
```

```python
import functools
import math

import jax
import jax.numpy as jnp
from jax import lax
from jax.experimental import pallas as pl
from jax.experimental.pallas import tpu as pltpu
from jax.sharding import PartitionSpec as P

HD = 128
D = 1024
T = 512
HALF = 256
BACK = 3
WINDOW = 1536
USERS = 4
EPS = 1e-06
SCALE = 1.0 / math.sqrt(HD)
MESH = pl.DeviceIdType.MESH
NT = (((1,), (1,)), ((), ()))
NN = (((1,), (0,)), ((), ()))
TN = (((0,), (0,)), ((), ()))
F32 = jnp.float32
BF16 = jnp.bfloat16


def dot(a, b, dims):
    return lax.dot_general(a, b, dims, preferred_element_type=F32)


def dot_exact(a, b, dims):
    return lax.dot_general(a, b, dims, preferred_element_type=F32, precision=lax.Precision.HIGHEST)


def query_bounds(pos, lengths, cands):
    seg = jnp.zeros_like(pos)
    cand = jnp.zeros_like(pos)
    start = jnp.int32(0)
    for u in range(USERS):
        length = lengths[u]
        end = start + length
        first = end - jnp.minimum(cands[u], length)
        inside = (pos >= start) & (pos < end)
        seg = jnp.where(inside, start, seg)
        cand = jnp.where(inside, first, cand)
        start = end
    return jnp.maximum(seg, pos - (WINDOW - 1)), jnp.minimum(cand, pos)


def weights(prod, allowed):
    h = prod * (0.5 * SCALE)
    w = 1.0 + jnp.tanh(h)
    a = jnp.where(allowed, w * (1.0 / WINDOW), 0.0)
    attn = (h * a).astype(BF16)
    slope = a * (0.5 + h * (1.0 - 0.5 * w))
    return attn, slope


def spans_q(d):
    if d == 0:
        return ((0, 0, HALF), (1, 0, T))
    if d == BACK:
        return ((0, 0, T), (1, HALF, HALF))
    return ((0, 0, T), (1, 0, T))


def spans_k(d):
    if d == 0:
        return ((0, 0, T), (1, HALF, HALF))
    if d == BACK:
        return ((0, 0, HALF), (1, 0, T))
    return ((0, 0, T), (1, 0, T))


def kernel(
    len_ref, cand_ref, gain_ref, q_hbm, k_hbm, v_hbm, gate_hbm, og_hbm,
    out_ref, dq_ref, dk_ref, dv_ref, dgate_ref,
    kbuf, vbuf, qbuf, dbuf, gate, og, mixed, dkacc, dvacc, back,
    slope_q, attn_k, slope_k, lo_q, hi_q, lo_k, hi_k, stats, gains,
    home_s, home_r, kv_s, kv_r, q_s, q_r, d_s, d_r, st_s, st_r, gain_s, gain_r, back_s, back_r,
):
    c = lax.axis_index("ctx")
    head = lax.axis_index("head")
    x = lax.rem(c, 4)
    core = lax.rem(head, 2)
    half = lax.rem(x, 2)
    side = x // 2
    first = c - x + 2 * core

    def device(row, place, which):
        return {"ctx": lax.rem(c - x + place + 4 * row + 128, 128), "head": head - core + which}

    partner = device(0, x, 1 - core)
    across = {"ctx": c, "head": lax.rem(head + 2, 4)}
    chips = [device(0, lax.rem(x + e, 4), core) for e in (1, 2, 3)]
    others = [device(0, lax.rem(x + e, 4), 1 - core) for e in (1, 2, 3)]
    rows = [device(r, x, k) for r in (1, -1) for k in (0, 1)]
    peers = [partner, across] + chips + others + rows
    bar = pltpu.get_barrier_semaphore()
    for p in peers:
        pl.semaphore_signal(bar, inc=1, device_id=p, device_id_type=MESH)
    pl.semaphore_wait(bar, len(peers))

    def remote(src, dst, ss, rs, dev):
        return pltpu.make_async_remote_copy(src, dst, ss, rs, device_id=dev, device_id_type=MESH)

    homes = ((k_hbm, kbuf, 3), (v_hbm, vbuf, 3), (q_hbm, qbuf, 0), (gate_hbm, gate, 0), (og_hbm, og, 0))

    def home(i, k, act):
        src, dst, base = homes[i]
        src = src.at[:, pl.ds(k * HD, HD)]
        dst = dst.at[base + half]

        @pl.when(2 * core + k != x)
        def _():
            act(remote(src, dst, home_s.at[i, k], home_r.at[i, half], device(0, 2 * core + k, side)))

    def home_local(i, k):
        src, dst, base = homes[i]

        @pl.when(2 * core + k == x)
        def _():
            pltpu.make_async_copy(src.at[:, pl.ds(k * HD, HD)], dst.at[base + half], home_r.at[i, half]).start()

    def home_wait(i, b):
        _, dst, base = homes[i]
        remote(dst.at[base + b], dst.at[base + b], home_s.at[i, 0], home_r.at[i, b], partner).wait_recv()

    for i in range(5):
        for k in range(2):
            home(i, k, lambda cp: cp.start())
            home_local(i, k)
    gains[0] = jnp.broadcast_to(gain_ref[...].astype(F32).reshape(1, 2 * HD), (8, 2 * HD))
    gain_copy = remote(gains.at[0], gains.at[1], gain_s, gain_r, partner)
    gain_copy.start()

    kv_routes = (
        (0, 0, 3, partner, 1), (0, 1, 4, partner, 2), (0, 2, 4, device(1, x, 0), 0),
        (1, 0, 3, device(1, x, 0), 1), (1, 1, 4, device(1, x, 1), 0), (1, 2, 0, partner, 2),
    )
    q_routes = (
        (0, 0, 0, device(-1, x, 1), 2), (0, 1, 1, device(-1, x, 1), 3),
        (1, 0, 0, partner, 2), (1, 1, 0, device(-1, x, 1), 4), (1, 2, 1, partner, 3), (1, 3, 2, partner, 4),
    )

    def pass_on(routes, buf, ss, rs, wanted, act):
        for which in range(2):
            todo = [r for r in routes if r[0] == which and r[2] in wanted]
            if todo:

                @pl.when(core == which)
                def _():
                    for _, number, at, to, slot in todo:
                        act(remote(buf.at[at], buf.at[slot], ss.at[number], rs.at[slot], to))

    def kv_pass(a, *wanted):
        pass_on(kv_routes, (kbuf, vbuf)[a], kv_s.at[a], kv_r.at[a], wanted, lambda cp: cp.start())

    def q_pass(*wanted):
        pass_on(q_routes, qbuf, q_s, q_r, wanted, lambda cp: cp.start())

    def d_pass(*wanted):
        pass_on(q_routes, dbuf, d_s, d_r, wanted, lambda cp: cp.start())

    def slot_wait(buf, ss, rs, slot):
        remote(buf.at[slot], buf.at[slot], ss.at[0], rs.at[slot], partner).wait_recv()

    def kv_wait(w):
        for a in range(2):
            slot_wait((kbuf, vbuf)[a], kv_s.at[a], kv_r.at[a], w)

    for b in range(2):
        pos = (first + b) * T + lax.broadcasted_iota(jnp.int32, (T, HD), 0)
        lo_q[b], hi_q[b] = query_bounds(pos, len_ref, cand_ref)
    for u in range(BACK + 2):
        pos = (first + u) * T + lax.broadcasted_iota(jnp.int32, (8, T), 1)
        lo_k[u], hi_k[u] = query_bounds(pos, len_ref, cand_ref)

    def forward(b, d):
        w = BACK + b - d
        for t, k0, kn in spans_q(d):
            r = pl.ds(t * HALF, HALF)
            prod = dot(qbuf[b, r, :], kbuf[w, pl.ds(k0, kn), :], NT)
            key = (first + b - d) * T + k0 + lax.broadcasted_iota(jnp.int32, (HALF, kn), 1)
            lo = jnp.concatenate([lo_q[b, r, :]] * (kn // HD), axis=1)
            hi = jnp.concatenate([hi_q[b, r, :]] * (kn // HD), axis=1)
            allowed = (key >= lo) & (key < hi)
            if d == 0:
                own = (first + b) * T + t * HALF + lax.broadcasted_iota(jnp.int32, (HALF, kn), 0)
                allowed = allowed | (key == own)
            attn, slope = weights(prod, allowed)
            slope_q[b, r, pl.ds(d * T + k0, kn)] = slope
            part = dot(attn, vbuf[w, pl.ds(k0, kn), :], NN)
            mixed[b, r, :] = part if d == 0 else mixed[b, r, :] + part

    def keys_before(b, d):
        u = b + d
        for t, q0, qn in spans_k(d):
            r = pl.ds(t * HALF, HALF)
            prod = dot(kbuf[BACK + b, r, :], qbuf[u, pl.ds(q0, qn), :], NT)
            key = (first + b) * T + t * HALF + lax.broadcasted_iota(jnp.int32, (HALF, qn), 0)
            allowed = (key >= lo_k[u, 0:1, pl.ds(q0, qn)]) & (key < hi_k[u, 0:1, pl.ds(q0, qn)])
            if d == 0:
                own = (first + b) * T + q0 + lax.broadcasted_iota(jnp.int32, (HALF, qn), 1)
                allowed = allowed | (key == own)
            attn, slope = weights(prod, allowed)
            attn_k[b, r, pl.ds(d * T + q0, qn)] = attn
            slope_k[b, r, pl.ds(d * T + q0, qn)] = slope

    def keys_after(b, d):
        u = b + d
        for t, q0, qn in spans_k(d):
            r = pl.ds(t * HALF, HALF)
            dm = dbuf[u, pl.ds(q0, qn), :]
            part = dot(attn_k[b, r, pl.ds(d * T + q0, qn)], dm, NN)
            dvacc[b, r, :] = part if d == 0 else dvacc[b, r, :] + part
            dattn = dot(vbuf[BACK + b, r, :], dm, NT)
            dscore = (dattn * slope_k[b, r, pl.ds(d * T + q0, qn)]).astype(BF16)
            part = dot(dscore, qbuf[u, pl.ds(q0, qn), :], NN)
            dkacc[b, r, :] = part if d == 0 else dkacc[b, r, :] + part

    def query_grad(b):
        for t in range(2):
            r = pl.ds(t * HALF, HALF)
            dm = dbuf[b, r, :]
            total = jnp.zeros((HALF, HD), F32)
            for d in range(BACK + 1):
                w = BACK + b - d
                _, k0, kn = spans_q(d)[t]
                dattn = dot(dm, vbuf[w, pl.ds(k0, kn), :], NT)
                dscore = (dattn * slope_q[b, r, pl.ds(d * T + k0, kn)]).astype(BF16)
                total += dot(dscore, kbuf[w, pl.ds(k0, kn), :], NN)
            back[1, b, r, :] = (total * SCALE).astype(BF16)

    finals = (out_ref, dq_ref, dk_ref, dv_ref, dgate_ref)

    def back_copy(i, b, act):
        dst = finals[i].at[:, pl.ds(pl.multiple_of(half * HD, HD), HD)]

        @pl.when(2 * core + b != x)
        def _():
            act(remote(back.at[i, b], dst, back_s.at[i, b], back_r.at[i, half], device(0, 2 * core + b, side)))

    def send_back(i, b):
        back_copy(i, b, lambda cp: cp.start())
        dst = finals[i].at[:, pl.ds(pl.multiple_of(half * HD, HD), HD)]

        @pl.when(2 * core + b == x)
        def _():
            pltpu.make_async_copy(back.at[i, b], dst, back_r.at[i, half]).start()

    for b in range(2):
        for a in range(2):
            home_wait(a, b)
            kv_pass(a, BACK + b)
    for b in range(2):
        home_wait(2, b)
        q_pass(b)
    forward(0, 0)
    forward(1, 0)
    forward(1, 1)

    @pl.when(core == 1)
    def _():
        kv_wait(0)

    for a in range(2):
        pass_on(kv_routes, (kbuf, vbuf)[a], kv_s.at[a], kv_r.at[a], (0,), lambda cp: cp.start())
    kv_wait(1)
    forward(0, 2)
    forward(1, 3)

    @pl.when(core == 0)
    def _():
        kv_wait(0)

    forward(0, 3)
    kv_wait(2)
    forward(0, 1)
    forward(1, 2)

    gain_copy.wait_recv()
    for i in (3, 4):
        for b in range(2):
            home_wait(i, b)
    gain = jnp.where(core == side, gains[0], gains[1])
    gain = jnp.where(half == 0, gain[0:1, :HD], gain[0:1, HD:])
    pick = lax.broadcasted_iota(jnp.int32, (8, HD), 0)
    total = jnp.zeros((8, T), F32)
    for b in range(2):
        m = mixed[b]
        dnorm = og[b].astype(F32) * gate[b].astype(F32) * gain
        for i, a in enumerate((m, m * m, dnorm, dnorm * m)):
            total += dot_exact((pick == 4 * b + i).astype(F32), a, NT)
    stats[0] = total

    def st(e):
        return remote(stats.at[0], stats.at[e], st_s.at[e - 1], st_r.at[e - 1], chips[e - 1])

    for e in range(1, 4):
        st(e).start()
    keys_before(0, 0)
    keys_before(1, 0)
    for e in range(1, 4):
        st(e).wait_recv()
    stats[4] = stats[0] + stats[1] + stats[2] + stats[3]
    st_across = remote(stats.at[4], stats.at[5], st_s.at[3], st_r.at[3], across)
    st_across.start()
    slot_wait(qbuf, q_s, q_r, 2)
    q_pass(2)
    keys_before(0, 1)
    keys_before(0, 2)
    keys_before(1, 1)
    st_across.wait_recv()
    total = stats[4] + stats[5]
    for b in range(2):
        sums = total[4 * b : 4 * b + 4]
        mean = sums[0:1] / D
        var = sums[1:2] / D - mean * mean
        rstd = lax.rsqrt(var + EPS)
        mean_one = sums[2:3] / D
        mean_two = rstd * (sums[3:4] - mean * sums[2:3]) / D
        coef = jnp.concatenate([mean, rstd, mean_one, mean_two, jnp.zeros((4, T), F32)], axis=0)
        mean, rstd, mean_one, mean_two = [dot_exact(coef, (pick == i).astype(F32), TN) for i in range(4)]
        normed = (mixed[b] - mean) * rstd
        gf = gate[b].astype(F32)
        of = og[b].astype(F32)
        dbuf[b] = (rstd * (of * gf * gain - mean_one - normed * mean_two)).astype(BF16)
        d_pass(b)
        back[0, b] = (normed * gain * gf).astype(BF16)
        back[4, b] = (of * normed * gain).astype(BF16)
        send_back(0, b)
        send_back(4, b)
    query_grad(0)
    send_back(1, 0)
    slot_wait(dbuf, d_s, d_r, 2)
    d_pass(2)
    query_grad(1)
    send_back(1, 1)
    slot_wait(qbuf, q_s, q_r, 3)
    keys_before(0, 3)
    keys_before(1, 2)
    slot_wait(qbuf, q_s, q_r, 4)
    keys_before(1, 3)
    keys_after(0, 0)
    keys_after(1, 0)
    keys_after(0, 1)
    keys_after(0, 2)
    slot_wait(dbuf, d_s, d_r, 3)
    keys_after(0, 3)

    def finish_keys(b):
        back[2, b] = (dkacc[b] * SCALE).astype(BF16)
        back[3, b] = dvacc[b].astype(BF16)
        send_back(2, b)
        send_back(3, b)

    finish_keys(0)
    keys_after(1, 1)
    keys_after(1, 2)
    slot_wait(dbuf, d_s, d_r, 4)
    keys_after(1, 3)
    finish_keys(1)

    for e in range(1, 4):
        st(e).wait_send()
    st_across.wait_send()
    gain_copy.wait_send()
    done = lambda cp: cp.wait_send()
    for a in range(2):
        pass_on(kv_routes, (kbuf, vbuf)[a], kv_s.at[a], kv_r.at[a], range(5), done)
    pass_on(q_routes, qbuf, q_s, q_r, range(5), done)
    pass_on(q_routes, dbuf, d_s, d_r, range(5), done)
    for i in range(5):
        for k in range(2):
            home(i, k, done)
            back_copy(i, k, done)
            dst = finals[i].at[:, pl.ds(k * HD, HD)]
            remote(back.at[i, k], dst, back_s.at[i, k], back_r.at[i, k], partner).wait_recv()


def write_out(*refs):
    src, dst, buf, into, out = refs[:5], refs[5:10], *refs[10:]
    reads = [pltpu.make_async_copy(src[i], buf.at[i], into.at[i]) for i in range(5)]
    writes = [pltpu.make_async_copy(buf.at[i], dst[i], out.at[i]) for i in range(5)]
    for cp in reads:
        cp.start()
    for read, write in zip(reads, writes):
        read.wait()
        write.start()
    for cp in writes:
        cp.wait()


def per_device(queries, key_rows, value_rows, gating, gain_vector, out_grad, user_lengths, cand_counts):
    feat = queries.shape[1]
    block = jax.ShapeDtypeStruct((T, feat), BF16)
    vmem = pl.BlockSpec(memory_space=pltpu.VMEM)
    smem = pl.BlockSpec(memory_space=pltpu.SMEM)
    hbm = pl.BlockSpec(memory_space=pltpu.HBM)
    sem = pltpu.SemaphoreType.DMA
    results = pl.pallas_call(
        kernel,
        out_shape=[block] * 5,
        in_specs=[smem, smem, vmem, hbm, hbm, hbm, hbm, hbm],
        out_specs=[hbm] * 5,
        scratch_shapes=[
            pltpu.VMEM((5, T, HD), BF16),
            pltpu.VMEM((5, T, HD), BF16),
            pltpu.VMEM((5, T, HD), BF16),
            pltpu.VMEM((5, T, HD), BF16),
            pltpu.VMEM((2, T, HD), BF16),
            pltpu.VMEM((2, T, HD), BF16),
            pltpu.VMEM((2, T, HD), F32),
            pltpu.VMEM((2, T, HD), F32),
            pltpu.VMEM((2, T, HD), F32),
            pltpu.VMEM((5, 2, T, HD), BF16),
            pltpu.VMEM((2, T, 4 * T), F32),
            pltpu.VMEM((2, T, 4 * T), BF16),
            pltpu.VMEM((2, T, 4 * T), F32),
            pltpu.VMEM((2, T, HD), jnp.int32),
            pltpu.VMEM((2, T, HD), jnp.int32),
            pltpu.VMEM((5, 8, T), jnp.int32),
            pltpu.VMEM((5, 8, T), jnp.int32),
            pltpu.VMEM((6, 8, T), F32),
            pltpu.VMEM((2, 8, 2 * HD), F32),
            sem((5, 2)), sem((5, 2)),
            sem((2, 3)), sem((2, 3)),
            sem((4,)), sem((5,)),
            sem((4,)), sem((5,)),
            sem((4,)), sem((4,)),
            sem, sem,
            sem((5, 2)), sem((5, 2)),
        ],
        compiler_params=pltpu.CompilerParams(
            collective_id=0, has_side_effects=True, vmem_limit_bytes=61 << 20
        ),
        name="hstu",
    )(user_lengths, cand_counts, gain_vector, queries, key_rows, value_rows, gating, out_grad)
    return pl.pallas_call(
        write_out,
        out_shape=[block] * 5,
        in_specs=[hbm] * 5,
        out_specs=[hbm] * 5,
        scratch_shapes=[pltpu.VMEM((5, T, feat), BF16), sem((5,)), sem((5,))],
        name="write_out",
    )(*results)


def solution(mesh):
    tokens = P("ctx", "head")
    return jax.shard_map(
        per_device,
        mesh=mesh,
        in_specs=(tokens, tokens, tokens, tokens, P("head"), tokens, P(), P()),
        out_specs=(tokens,) * 5,
        check_vma=False,
    )
```

```python
import functools
import math

import jax
import jax.numpy as jnp
from jax import lax
from jax.experimental import pallas as pl
from jax.experimental.pallas import tpu as pltpu
from jax.sharding import PartitionSpec as P

HD = 128
D = 1024
T = 512
HALF = 256
BACK = 3
WINDOW = 1536
USERS = 4
EPS = 1e-06
SCALE = 1.0 / math.sqrt(HD)
MESH = pl.DeviceIdType.MESH
NT = (((1,), (1,)), ((), ()))
NN = (((1,), (0,)), ((), ()))
TN = (((0,), (0,)), ((), ()))
F32 = jnp.float32
BF16 = jnp.bfloat16


def dot(a, b, dims):
    return lax.dot_general(a, b, dims, preferred_element_type=F32)


def dot_exact(a, b, dims):
    return lax.dot_general(a, b, dims, preferred_element_type=F32, precision=lax.Precision.HIGHEST)


def query_bounds(pos, lengths, cands):
    seg = jnp.zeros_like(pos)
    cand = jnp.zeros_like(pos)
    start = jnp.int32(0)
    for u in range(USERS):
        length = lengths[u]
        end = start + length
        first = end - jnp.minimum(cands[u], length)
        inside = (pos >= start) & (pos < end)
        seg = jnp.where(inside, start, seg)
        cand = jnp.where(inside, first, cand)
        start = end
    return jnp.maximum(seg, pos - (WINDOW - 1)), jnp.minimum(cand, pos)


def weights(prod, allowed):
    h = prod * (0.5 * SCALE)
    w = 1.0 + jnp.tanh(h)
    a = jnp.where(allowed, w * (1.0 / WINDOW), 0.0)
    attn = (h * a).astype(BF16)
    slope = a * (0.5 + h * (1.0 - 0.5 * w))
    return attn, slope


def spans_q(d):
    if d == 0:
        return ((0, 0, HALF), (1, 0, T))
    if d == BACK:
        return ((0, 0, T), (1, HALF, HALF))
    return ((0, 0, T), (1, 0, T))


def spans_k(d):
    if d == 0:
        return ((0, 0, T), (1, HALF, HALF))
    if d == BACK:
        return ((0, 0, HALF), (1, 0, T))
    return ((0, 0, T), (1, 0, T))


def kernel(
    len_ref, cand_ref, gain_ref, q_hbm, k_hbm, v_hbm, gate_hbm, og_hbm,
    out_ref, dq_ref, dk_ref, dv_ref, dgate_ref,
    kbuf, vbuf, qbuf, dbuf, gate, og, mixed, dkacc, dvacc, back, placed,
    slope_q, attn_k, slope_k, lo_q, hi_q, lo_k, hi_k, stats, gains,
    home_s, home_r, kv_s, kv_r, q_s, q_r, d_s, d_r, st_s, st_r, gain_s, gain_r, back_s, back_r, own,
):
    c = lax.axis_index("ctx")
    head = lax.axis_index("head")
    x = lax.rem(c, 4)
    core = lax.rem(head, 2)
    half = lax.rem(x, 2)
    side = x // 2
    first = c - x + 2 * core

    def device(row, place, which):
        return {"ctx": lax.rem(c - x + place + 4 * row + 128, 128), "head": head - core + which}

    partner = device(0, x, 1 - core)
    across = {"ctx": c, "head": lax.rem(head + 2, 4)}
    chips = [device(0, lax.rem(x + e, 4), core) for e in (1, 2, 3)]
    others = [device(0, lax.rem(x + e, 4), 1 - core) for e in (1, 2, 3)]
    rows = [device(r, x, k) for r in (1, -1) for k in (0, 1)]
    peers = [partner, across] + chips + others + rows
    bar = pltpu.get_barrier_semaphore()
    for p in peers:
        pl.semaphore_signal(bar, inc=1, device_id=p, device_id_type=MESH)
    pl.semaphore_wait(bar, len(peers))

    def remote(src, dst, ss, rs, dev):
        return pltpu.make_async_remote_copy(src, dst, ss, rs, device_id=dev, device_id_type=MESH)

    homes = ((k_hbm, kbuf, 3), (v_hbm, vbuf, 3), (q_hbm, qbuf, 0), (gate_hbm, gate, 0), (og_hbm, og, 0))

    def home(i, k, act):
        src, dst, base = homes[i]
        src = src.at[:, pl.ds(k * HD, HD)]
        dst = dst.at[base + half]

        @pl.when(2 * core + k != x)
        def _():
            act(remote(src, dst, home_s.at[i, k], home_r.at[i, half], device(0, 2 * core + k, side)))

    def home_local(i, k):
        src, dst, base = homes[i]

        @pl.when(2 * core + k == x)
        def _():
            pltpu.make_async_copy(src.at[:, pl.ds(k * HD, HD)], dst.at[base + half], home_r.at[i, half]).start()

    def home_wait(i, b):
        _, dst, base = homes[i]
        remote(dst.at[base + b], dst.at[base + b], home_s.at[i, 0], home_r.at[i, b], partner).wait_recv()

    for i in range(5):
        for k in range(2):
            home(i, k, lambda cp: cp.start())
            home_local(i, k)
    owns = [pltpu.make_async_copy(ref, placed.at[i], own.at[i]) for i, ref in ((1, gate_hbm), (2, og_hbm))]
    for cp in owns:
        cp.start()
    gains[0] = jnp.broadcast_to(gain_ref[...].astype(F32).reshape(1, 2 * HD), (8, 2 * HD))
    gain_copy = remote(gains.at[0], gains.at[1], gain_s, gain_r, partner)
    gain_copy.start()

    kv_routes = (
        (0, 0, 3, partner, 1), (0, 1, 4, partner, 2), (0, 2, 4, device(1, x, 0), 0),
        (1, 0, 3, device(1, x, 0), 1), (1, 1, 4, device(1, x, 1), 0), (1, 2, 0, partner, 2),
    )
    q_routes = (
        (0, 0, 0, device(-1, x, 1), 2), (0, 1, 1, device(-1, x, 1), 3),
        (1, 0, 0, partner, 2), (1, 1, 0, device(-1, x, 1), 4), (1, 2, 1, partner, 3), (1, 3, 2, partner, 4),
    )

    def pass_on(routes, buf, ss, rs, wanted, act):
        for which in range(2):
            todo = [r for r in routes if r[0] == which and r[2] in wanted]
            if todo:

                @pl.when(core == which)
                def _():
                    for _, number, at, to, slot in todo:
                        act(remote(buf.at[at], buf.at[slot], ss.at[number], rs.at[slot], to))

    def kv_pass(a, *wanted):
        pass_on(kv_routes, (kbuf, vbuf)[a], kv_s.at[a], kv_r.at[a], wanted, lambda cp: cp.start())

    def q_pass(*wanted):
        pass_on(q_routes, qbuf, q_s, q_r, wanted, lambda cp: cp.start())

    def d_pass(*wanted):
        pass_on(q_routes, dbuf, d_s, d_r, wanted, lambda cp: cp.start())

    def slot_wait(buf, ss, rs, slot):
        remote(buf.at[slot], buf.at[slot], ss.at[0], rs.at[slot], partner).wait_recv()

    def kv_wait(w):
        for a in range(2):
            slot_wait((kbuf, vbuf)[a], kv_s.at[a], kv_r.at[a], w)

    for b in range(2):
        pos = (first + b) * T + lax.broadcasted_iota(jnp.int32, (T, HD), 0)
        lo_q[b], hi_q[b] = query_bounds(pos, len_ref, cand_ref)
    for u in range(BACK + 2):
        pos = (first + u) * T + lax.broadcasted_iota(jnp.int32, (8, T), 1)
        lo_k[u], hi_k[u] = query_bounds(pos, len_ref, cand_ref)

    def forward(b, d):
        w = BACK + b - d
        for t, k0, kn in spans_q(d):
            r = pl.ds(t * HALF, HALF)
            prod = dot(qbuf[b, r, :], kbuf[w, pl.ds(k0, kn), :], NT)
            key = (first + b - d) * T + k0 + lax.broadcasted_iota(jnp.int32, (HALF, kn), 1)
            lo = jnp.concatenate([lo_q[b, r, :]] * (kn // HD), axis=1)
            hi = jnp.concatenate([hi_q[b, r, :]] * (kn // HD), axis=1)
            allowed = (key >= lo) & (key < hi)
            if d == 0:
                own = (first + b) * T + t * HALF + lax.broadcasted_iota(jnp.int32, (HALF, kn), 0)
                allowed = allowed | (key == own)
            attn, slope = weights(prod, allowed)
            slope_q[b, r, pl.ds(d * T + k0, kn)] = slope
            part = dot(attn, vbuf[w, pl.ds(k0, kn), :], NN)
            mixed[b, r, :] = part if d == 0 else mixed[b, r, :] + part

    def keys_before(b, d):
        u = b + d
        for t, q0, qn in spans_k(d):
            r = pl.ds(t * HALF, HALF)
            prod = dot(kbuf[BACK + b, r, :], qbuf[u, pl.ds(q0, qn), :], NT)
            key = (first + b) * T + t * HALF + lax.broadcasted_iota(jnp.int32, (HALF, qn), 0)
            allowed = (key >= lo_k[u, 0:1, pl.ds(q0, qn)]) & (key < hi_k[u, 0:1, pl.ds(q0, qn)])
            if d == 0:
                own = (first + b) * T + q0 + lax.broadcasted_iota(jnp.int32, (HALF, qn), 1)
                allowed = allowed | (key == own)
            attn, slope = weights(prod, allowed)
            attn_k[b, r, pl.ds(d * T + q0, qn)] = attn
            slope_k[b, r, pl.ds(d * T + q0, qn)] = slope

    def keys_after(b, d):
        u = b + d
        for t, q0, qn in spans_k(d):
            r = pl.ds(t * HALF, HALF)
            dm = dbuf[u, pl.ds(q0, qn), :]
            part = dot(attn_k[b, r, pl.ds(d * T + q0, qn)], dm, NN)
            dvacc[b, r, :] = part if d == 0 else dvacc[b, r, :] + part
            dattn = dot(vbuf[BACK + b, r, :], dm, NT)
            dscore = (dattn * slope_k[b, r, pl.ds(d * T + q0, qn)]).astype(BF16)
            part = dot(dscore, qbuf[u, pl.ds(q0, qn), :], NN)
            dkacc[b, r, :] = part if d == 0 else dkacc[b, r, :] + part

    def query_grad(b):
        for t in range(2):
            r = pl.ds(t * HALF, HALF)
            dm = dbuf[b, r, :]
            total = jnp.zeros((HALF, HD), F32)
            for d in range(BACK + 1):
                w = BACK + b - d
                _, k0, kn = spans_q(d)[t]
                dattn = dot(dm, vbuf[w, pl.ds(k0, kn), :], NT)
                dscore = (dattn * slope_q[b, r, pl.ds(d * T + k0, kn)]).astype(BF16)
                total += dot(dscore, kbuf[w, pl.ds(k0, kn), :], NN)
            back[1, b, r, :] = (total * SCALE).astype(BF16)

    finals = (placed.at[0], dq_ref, dk_ref, dv_ref)

    def back_copy(i, b, act):
        dst = finals[i].at[:, pl.ds(pl.multiple_of(half * HD, HD), HD)]

        @pl.when(2 * core + b != x)
        def _():
            act(remote(back.at[i, b], dst, back_s.at[i, b], back_r.at[i, half], device(0, 2 * core + b, side)))

    def send_back(i, b):
        back_copy(i, b, lambda cp: cp.start())
        dst = finals[i].at[:, pl.ds(pl.multiple_of(half * HD, HD), HD)]

        @pl.when(2 * core + b == x)
        def _():
            pltpu.make_async_copy(back.at[i, b], dst, back_r.at[i, half]).start()

    for a in range(2):
        for b in range(2):
            home_wait(a, b)
            kv_pass(a, BACK + b)
    for b in range(2):
        home_wait(2, b)
        q_pass(b)
    forward(0, 0)
    forward(1, 0)
    forward(1, 1)
    kv_wait(1)
    forward(0, 2)
    forward(1, 3)

    @pl.when(core == 1)
    def _():
        kv_wait(0)

    for a in range(2):
        pass_on(kv_routes, (kbuf, vbuf)[a], kv_s.at[a], kv_r.at[a], (0,), lambda cp: cp.start())
    keys_before(0, 0)

    @pl.when(core == 0)
    def _():
        kv_wait(0)

    forward(0, 3)
    kv_wait(2)
    forward(0, 1)
    forward(1, 2)

    gain_copy.wait_recv()
    gain = jnp.where(core == side, gains[0], gains[1])
    gain = jnp.where(half == 0, gain[0:1, :HD], gain[0:1, HD:])
    pick = lax.broadcasted_iota(jnp.int32, (8, HD), 0)

    def st(e):
        return remote(stats.at[0], stats.at[e], st_s.at[e - 1], st_r.at[e - 1], chips[e - 1])

    st_across = remote(stats.at[4], stats.at[5], st_s.at[3], st_r.at[3], across)

    def sums_along():
        for i in (3, 4):
            for b in range(2):
                home_wait(i, b)
        total = jnp.zeros((8, T), F32)
        for b in range(2):
            m = mixed[b]
            dnorm = og[b].astype(F32) * gate[b].astype(F32) * gain
            for i, a in enumerate((m, m * m, dnorm, dnorm * m)):
                total += dot_exact((pick == 4 * b + i).astype(F32), a, NT)
        stats[0] = total
        for e in range(1, 4):
            st(e).start()

    def sums_across():
        for e in range(1, 4):
            st(e).wait_recv()
        stats[4] = stats[0] + stats[1] + stats[2] + stats[3]
        st_across.start()

    def norm():
        st_across.wait_recv()
        total = stats[4] + stats[5]
        for b in range(2):
            sums = total[4 * b : 4 * b + 4]
            mean = sums[0:1] / D
            var = sums[1:2] / D - mean * mean
            rstd = lax.rsqrt(var + EPS)
            mean_one = sums[2:3] / D
            mean_two = rstd * (sums[3:4] - mean * sums[2:3]) / D
            coef = jnp.concatenate([mean, rstd, mean_one, mean_two, jnp.zeros((4, T), F32)], axis=0)
            mean, rstd, mean_one, mean_two = [dot_exact(coef, (pick == i).astype(F32), TN) for i in range(4)]
            normed = (mixed[b] - mean) * rstd
            dnorm = og[b].astype(F32) * gate[b].astype(F32) * gain
            dbuf[b] = (rstd * (dnorm - mean_one - normed * mean_two)).astype(BF16)
            d_pass(b)
            back[0, b] = normed.astype(BF16)
        for b in range(2):
            send_back(0, b)

    def back_wait(i):
        for k in range(2):
            dst = finals[i].at[:, pl.ds(k * HD, HD)]
            remote(back.at[i, k], dst, back_s.at[i, k], back_r.at[i, k], partner).wait_recv()

    writes = [pltpu.make_async_copy(placed.at[i], ref, own.at[i]) for i, ref in ((3, out_ref), (4, dgate_ref))]

    def gated():
        back_wait(0)
        for cp in owns:
            cp.wait()
        normed = placed[0].astype(F32)
        gain = gains[0, 0:1, :]
        placed[3] = (normed * gain * placed[1].astype(F32)).astype(BF16)
        placed[4] = (placed[2].astype(F32) * normed * gain).astype(BF16)
        for cp in writes:
            cp.start()

    def finish_keys(b):
        back[2, b] = (dkacc[b] * SCALE).astype(BF16)
        back[3, b] = dvacc[b].astype(BF16)
        send_back(2, b)
        send_back(3, b)

    sums_along()
    keys_before(1, 0)
    keys_before(0, 1)
    sums_across()
    slot_wait(qbuf, q_s, q_r, 2)
    q_pass(2)
    keys_before(0, 2)
    keys_before(1, 1)
    slot_wait(qbuf, q_s, q_r, 3)
    keys_before(0, 3)
    keys_before(1, 2)
    slot_wait(qbuf, q_s, q_r, 4)
    keys_before(1, 3)
    norm()
    keys_after(0, 0)
    keys_after(1, 0)
    keys_after(0, 1)
    query_grad(0)
    send_back(1, 0)
    slot_wait(dbuf, d_s, d_r, 2)
    d_pass(2)
    keys_after(0, 2)
    keys_after(1, 1)
    slot_wait(dbuf, d_s, d_r, 3)
    keys_after(0, 3)
    finish_keys(0)
    query_grad(1)
    send_back(1, 1)
    keys_after(1, 2)
    gated()
    slot_wait(dbuf, d_s, d_r, 4)
    keys_after(1, 3)
    finish_keys(1)

    for e in range(1, 4):
        st(e).wait_send()
    st_across.wait_send()
    gain_copy.wait_send()
    done = lambda cp: cp.wait_send()
    for a in range(2):
        pass_on(kv_routes, (kbuf, vbuf)[a], kv_s.at[a], kv_r.at[a], range(5), done)
    pass_on(q_routes, qbuf, q_s, q_r, range(5), done)
    pass_on(q_routes, dbuf, d_s, d_r, range(5), done)
    for i in range(5):
        for k in range(2):
            home(i, k, done)
            if i < 4:
                back_copy(i, k, done)
    for i in (1, 2, 3):
        back_wait(i)
    for cp in writes:
        cp.wait()


def write_out(*refs):
    src, dst, buf, into, out = refs[:5], refs[5:10], *refs[10:]
    reads = [pltpu.make_async_copy(src[i], buf.at[i], into.at[i]) for i in range(5)]
    writes = [pltpu.make_async_copy(buf.at[i], dst[i], out.at[i]) for i in range(5)]
    for cp in reads:
        cp.start()
    for read, write in zip(reads, writes):
        read.wait()
        write.start()
    for cp in writes:
        cp.wait()


def per_device(queries, key_rows, value_rows, gating, gain_vector, out_grad, user_lengths, cand_counts):
    feat = queries.shape[1]
    block = jax.ShapeDtypeStruct((T, feat), BF16)
    vmem = pl.BlockSpec(memory_space=pltpu.VMEM)
    smem = pl.BlockSpec(memory_space=pltpu.SMEM)
    hbm = pl.BlockSpec(memory_space=pltpu.HBM)
    sem = pltpu.SemaphoreType.DMA
    results = pl.pallas_call(
        kernel,
        out_shape=[block] * 5,
        in_specs=[smem, smem, vmem, hbm, hbm, hbm, hbm, hbm],
        out_specs=[hbm] * 5,
        scratch_shapes=[
            pltpu.VMEM((5, T, HD), BF16),
            pltpu.VMEM((5, T, HD), BF16),
            pltpu.VMEM((5, T, HD), BF16),
            pltpu.VMEM((5, T, HD), BF16),
            pltpu.VMEM((2, T, HD), BF16),
            pltpu.VMEM((2, T, HD), BF16),
            pltpu.VMEM((2, T, HD), F32),
            pltpu.VMEM((2, T, HD), F32),
            pltpu.VMEM((2, T, HD), F32),
            pltpu.VMEM((4, 2, T, HD), BF16),
            pltpu.VMEM((5, T, feat), BF16),
            pltpu.VMEM((2, T, 4 * T), F32),
            pltpu.VMEM((2, T, 4 * T), BF16),
            pltpu.VMEM((2, T, 4 * T), F32),
            pltpu.VMEM((2, T, HD), jnp.int32),
            pltpu.VMEM((2, T, HD), jnp.int32),
            pltpu.VMEM((5, 8, T), jnp.int32),
            pltpu.VMEM((5, 8, T), jnp.int32),
            pltpu.VMEM((6, 8, T), F32),
            pltpu.VMEM((2, 8, 2 * HD), F32),
            sem((5, 2)), sem((5, 2)),
            sem((2, 3)), sem((2, 3)),
            sem((4,)), sem((5,)),
            sem((4,)), sem((5,)),
            sem((4,)), sem((4,)),
            sem, sem,
            sem((4, 2)), sem((4, 2)),
            sem((5,)),
        ],
        compiler_params=pltpu.CompilerParams(
            collective_id=0, has_side_effects=True, vmem_limit_bytes=61 << 20
        ),
        name="hstu",
    )(user_lengths, cand_counts, gain_vector, queries, key_rows, value_rows, gating, out_grad)
    return pl.pallas_call(
        write_out,
        out_shape=[block] * 5,
        in_specs=[hbm] * 5,
        out_specs=[hbm] * 5,
        scratch_shapes=[pltpu.VMEM((5, T, feat), BF16), sem((5,)), sem((5,))],
        name="write_out",
    )(*results)


def solution(mesh):
    tokens = P("ctx", "head")
    return jax.shard_map(
        per_device,
        mesh=mesh,
        in_specs=(tokens, tokens, tokens, tokens, P("head"), tokens, P(), P()),
        out_specs=(tokens,) * 5,
        check_vma=False,
    )
```

```python
import functools
import math

import jax
import jax.numpy as jnp
from jax import lax
from jax.experimental import pallas as pl
from jax.experimental.pallas import tpu as pltpu
from jax.sharding import PartitionSpec as P

HD = 128
D = 1024
T = 512
HALF = 256
BACK = 3
WINDOW = 1536
USERS = 4
EPS = 1e-06
SCALE = 1.0 / math.sqrt(HD)
MESH = pl.DeviceIdType.MESH
NT = (((1,), (1,)), ((), ()))
NN = (((1,), (0,)), ((), ()))
TN = (((0,), (0,)), ((), ()))
F32 = jnp.float32
BF16 = jnp.bfloat16


def dot(a, b, dims):
    return lax.dot_general(a, b, dims, preferred_element_type=F32)


def dot_exact(a, b, dims):
    return lax.dot_general(a, b, dims, preferred_element_type=F32, precision=lax.Precision.HIGHEST)


def query_bounds(pos, lengths, cands):
    seg = jnp.zeros_like(pos)
    cand = jnp.zeros_like(pos)
    start = jnp.int32(0)
    for u in range(USERS):
        length = lengths[u]
        end = start + length
        first = end - jnp.minimum(cands[u], length)
        inside = (pos >= start) & (pos < end)
        seg = jnp.where(inside, start, seg)
        cand = jnp.where(inside, first, cand)
        start = end
    return jnp.maximum(seg, pos - (WINDOW - 1)), jnp.minimum(cand, pos)


def weights(prod, allowed):
    h = prod * (0.5 * SCALE)
    w = 1.0 + jnp.tanh(h)
    a = jnp.where(allowed, w * (1.0 / WINDOW), 0.0)
    attn = (h * a).astype(BF16)
    slope = a * (0.5 + h * (1.0 - 0.5 * w))
    return attn, slope


def spans_q(d):
    if d == 0:
        return ((0, 0, HALF), (1, 0, T))
    if d == BACK:
        return ((0, 0, T), (1, HALF, HALF))
    return ((0, 0, T), (1, 0, T))


def spans_k(d):
    if d == 0:
        return ((0, 0, T), (1, HALF, HALF))
    if d == BACK:
        return ((0, 0, HALF), (1, 0, T))
    return ((0, 0, T), (1, 0, T))


def kernel(
    len_ref, cand_ref, gain_ref, q_hbm, k_hbm, v_hbm, gate_hbm, og_hbm,
    out_ref, dq_ref, dk_ref, dv_ref, dgate_ref,
    kbuf, vbuf, qbuf, dbuf, gate, og, mixed, dkacc, dvacc, back, placed,
    slope_q, attn_k, slope_k, lo_q, hi_q, lo_k, hi_k, stats, gains,
    home_s, home_r, kv_s, kv_r, q_s, q_r, d_s, d_r, st_s, st_r, gain_s, gain_r, back_s, back_r, own,
):
    c = lax.axis_index("ctx")
    head = lax.axis_index("head")
    x = lax.rem(c, 4)
    core = lax.rem(head, 2)
    half = lax.rem(x, 2)
    side = x // 2
    first = c - x + 2 * core

    def device(row, place, which):
        return {"ctx": lax.rem(c - x + place + 4 * row + 128, 128), "head": head - core + which}

    partner = device(0, x, 1 - core)
    across = {"ctx": c, "head": lax.rem(head + 2, 4)}
    chips = [device(0, lax.rem(x + e, 4), core) for e in (1, 2, 3)]
    others = [device(0, lax.rem(x + e, 4), 1 - core) for e in (1, 2, 3)]
    rows = [device(r, x, k) for r in (1, -1) for k in (0, 1)]
    peers = [across] + rows + chips + others + [partner]
    bar = pltpu.get_barrier_semaphore()
    for p in peers:
        pl.semaphore_signal(bar, inc=1, device_id=p, device_id_type=MESH)
    pl.semaphore_wait(bar, len(peers))

    def remote(src, dst, ss, rs, dev):
        return pltpu.make_async_remote_copy(src, dst, ss, rs, device_id=dev, device_id_type=MESH)

    homes = ((k_hbm, kbuf, 3), (v_hbm, vbuf, 3), (q_hbm, qbuf, 0), (gate_hbm, gate, 0), (og_hbm, og, 0))

    def home(i, k, act):
        src, dst, base = homes[i]
        src = src.at[:, pl.ds(k * HD, HD)]
        dst = dst.at[base + half]

        @pl.when(2 * core + k != x)
        def _():
            act(remote(src, dst, home_s.at[i, k], home_r.at[i, half], device(0, 2 * core + k, side)))

    def home_local(i, k):
        src, dst, base = homes[i]

        @pl.when(2 * core + k == x)
        def _():
            pltpu.make_async_copy(src.at[:, pl.ds(k * HD, HD)], dst.at[base + half], home_r.at[i, half]).start()

    def home_wait(i, b):
        _, dst, base = homes[i]
        remote(dst.at[base + b], dst.at[base + b], home_s.at[i, 0], home_r.at[i, b], partner).wait_recv()

    for i in range(5):
        for k in range(2):
            home(i, k, lambda cp: cp.start())
            home_local(i, k)
    owns = [pltpu.make_async_copy(ref, placed.at[i], own.at[i]) for i, ref in ((1, gate_hbm), (2, og_hbm))]
    for cp in owns:
        cp.start()
    gains[0] = jnp.broadcast_to(gain_ref[...].astype(F32).reshape(1, 2 * HD), (8, 2 * HD))
    gain_copy = remote(gains.at[0], gains.at[1], gain_s, gain_r, partner)
    gain_copy.start()

    kv_routes = (
        (0, 0, 3, partner, 1), (0, 1, 4, partner, 2), (0, 2, 4, device(1, x, 0), 0),
        (1, 0, 3, device(1, x, 0), 1), (1, 1, 4, device(1, x, 1), 0), (1, 2, 0, partner, 2),
    )
    q_routes = (
        (0, 0, 0, device(-1, x, 1), 2), (0, 1, 1, device(-1, x, 1), 3),
        (1, 0, 0, partner, 2), (1, 1, 0, device(-1, x, 1), 4), (1, 2, 1, partner, 3), (1, 3, 2, partner, 4),
    )

    def pass_on(routes, buf, ss, rs, wanted, act):
        for which in range(2):
            todo = [r for r in routes if r[0] == which and r[2] in wanted]
            if todo:

                @pl.when(core == which)
                def _():
                    for _, number, at, to, slot in todo:
                        act(remote(buf.at[at], buf.at[slot], ss.at[number], rs.at[slot], to))

    def kv_pass(a, *wanted):
        pass_on(kv_routes, (kbuf, vbuf)[a], kv_s.at[a], kv_r.at[a], wanted, lambda cp: cp.start())

    def q_pass(*wanted):
        pass_on(q_routes, qbuf, q_s, q_r, wanted, lambda cp: cp.start())

    def d_pass(*wanted):
        pass_on(q_routes, dbuf, d_s, d_r, wanted, lambda cp: cp.start())

    def slot_wait(buf, ss, rs, slot):
        remote(buf.at[slot], buf.at[slot], ss.at[0], rs.at[slot], partner).wait_recv()

    def kv_wait(w):
        for a in range(2):
            slot_wait((kbuf, vbuf)[a], kv_s.at[a], kv_r.at[a], w)

    for b in range(2):
        pos = (first + b) * T + lax.broadcasted_iota(jnp.int32, (T, HD), 0)
        lo_q[b], hi_q[b] = query_bounds(pos, len_ref, cand_ref)
    for u in range(BACK + 2):
        pos = (first + u) * T + lax.broadcasted_iota(jnp.int32, (8, T), 1)
        lo_k[u], hi_k[u] = query_bounds(pos, len_ref, cand_ref)

    def forward(b, d):
        w = BACK + b - d
        for t, k0, kn in spans_q(d):
            r = pl.ds(t * HALF, HALF)
            prod = dot(qbuf[b, r, :], kbuf[w, pl.ds(k0, kn), :], NT)
            key = (first + b - d) * T + k0 + lax.broadcasted_iota(jnp.int32, (HALF, kn), 1)
            lo = jnp.concatenate([lo_q[b, r, :]] * (kn // HD), axis=1)
            hi = jnp.concatenate([hi_q[b, r, :]] * (kn // HD), axis=1)
            allowed = (key >= lo) & (key < hi)
            if d == 0:
                own = (first + b) * T + t * HALF + lax.broadcasted_iota(jnp.int32, (HALF, kn), 0)
                allowed = allowed | (key == own)
            attn, slope = weights(prod, allowed)
            slope_q[b, r, pl.ds(d * T + k0, kn)] = slope
            part = dot(attn, vbuf[w, pl.ds(k0, kn), :], NN)
            mixed[b, r, :] = part if d == 0 else mixed[b, r, :] + part

    def keys_before(b, d):
        u = b + d
        for t, q0, qn in spans_k(d):
            r = pl.ds(t * HALF, HALF)
            prod = dot(kbuf[BACK + b, r, :], qbuf[u, pl.ds(q0, qn), :], NT)
            key = (first + b) * T + t * HALF + lax.broadcasted_iota(jnp.int32, (HALF, qn), 0)
            allowed = (key >= lo_k[u, 0:1, pl.ds(q0, qn)]) & (key < hi_k[u, 0:1, pl.ds(q0, qn)])
            if d == 0:
                own = (first + b) * T + q0 + lax.broadcasted_iota(jnp.int32, (HALF, qn), 1)
                allowed = allowed | (key == own)
            attn, slope = weights(prod, allowed)
            attn_k[b, r, pl.ds(d * T + q0, qn)] = attn
            slope_k[b, r, pl.ds(d * T + q0, qn)] = slope

    def keys_after(b, d):
        u = b + d
        for t, q0, qn in spans_k(d):
            r = pl.ds(t * HALF, HALF)
            dm = dbuf[u, pl.ds(q0, qn), :]
            part = dot(attn_k[b, r, pl.ds(d * T + q0, qn)], dm, NN)
            dvacc[b, r, :] = part if d == 0 else dvacc[b, r, :] + part
            dattn = dot(vbuf[BACK + b, r, :], dm, NT)
            dscore = (dattn * slope_k[b, r, pl.ds(d * T + q0, qn)]).astype(BF16)
            part = dot(dscore, qbuf[u, pl.ds(q0, qn), :], NN)
            dkacc[b, r, :] = part if d == 0 else dkacc[b, r, :] + part

    def query_grad(b):
        for t in range(2):
            r = pl.ds(t * HALF, HALF)
            dm = dbuf[b, r, :]
            total = jnp.zeros((HALF, HD), F32)
            for d in range(BACK + 1):
                w = BACK + b - d
                _, k0, kn = spans_q(d)[t]
                dattn = dot(dm, vbuf[w, pl.ds(k0, kn), :], NT)
                dscore = (dattn * slope_q[b, r, pl.ds(d * T + k0, kn)]).astype(BF16)
                total += dot(dscore, kbuf[w, pl.ds(k0, kn), :], NN)
            back[1, b, r, :] = (total * SCALE).astype(BF16)

    finals = (placed.at[0], dq_ref, dk_ref, dv_ref)

    def back_copy(i, b, act):
        dst = finals[i].at[:, pl.ds(pl.multiple_of(half * HD, HD), HD)]

        @pl.when(2 * core + b != x)
        def _():
            act(remote(back.at[i, b], dst, back_s.at[i, b], back_r.at[i, half], device(0, 2 * core + b, side)))

    def send_back(i, b):
        back_copy(i, b, lambda cp: cp.start())
        dst = finals[i].at[:, pl.ds(pl.multiple_of(half * HD, HD), HD)]

        @pl.when(2 * core + b == x)
        def _():
            pltpu.make_async_copy(back.at[i, b], dst, back_r.at[i, half]).start()

    for a in range(2):
        for b in range(2):
            home_wait(a, b)
            kv_pass(a, BACK + b)
    for b in range(2):
        home_wait(2, b)
        q_pass(b)
    forward(0, 0)
    forward(1, 0)
    forward(1, 1)
    kv_wait(1)
    forward(0, 2)
    forward(1, 3)

    @pl.when(core == 1)
    def _():
        for a in range(2):
            buf = (kbuf, vbuf)[a]
            slot_wait(buf, kv_s.at[a], kv_r.at[a], 0)
            remote(buf.at[0], buf.at[2], kv_s.at[a, 2], kv_r.at[a, 2], partner).start()

    keys_before(0, 0)

    @pl.when(core == 0)
    def _():
        kv_wait(0)

    forward(0, 3)
    kv_wait(2)
    forward(0, 1)
    forward(1, 2)

    gain_copy.wait_recv()
    gain = jnp.where(core == side, gains[0], gains[1])
    gain = jnp.where(half == 0, gain[0:1, :HD], gain[0:1, HD:])
    pick = lax.broadcasted_iota(jnp.int32, (8, HD), 0)

    def st(e):
        return remote(stats.at[0], stats.at[e], st_s.at[e - 1], st_r.at[e - 1], chips[e - 1])

    st_across = remote(stats.at[4], stats.at[5], st_s.at[3], st_r.at[3], across)

    def sums_along():
        for i in (3, 4):
            for b in range(2):
                home_wait(i, b)
        total = jnp.zeros((8, T), F32)
        for b in range(2):
            m = mixed[b]
            dnorm = og[b].astype(F32) * gate[b].astype(F32) * gain
            for i, a in enumerate((m, m * m, dnorm, dnorm * m)):
                total += dot_exact((pick == 4 * b + i).astype(F32), a, NT)
        stats[0] = total
        for e in range(1, 4):
            st(e).start()

    def sums_across():
        for e in range(1, 4):
            st(e).wait_recv()
        stats[4] = stats[0] + stats[1] + stats[2] + stats[3]
        st_across.start()

    def norm():
        st_across.wait_recv()
        total = stats[4] + stats[5]
        for b in range(2):
            sums = total[4 * b : 4 * b + 4]
            mean = sums[0:1] / D
            var = sums[1:2] / D - mean * mean
            rstd = lax.rsqrt(var + EPS)
            mean_one = sums[2:3] / D
            mean_two = rstd * (sums[3:4] - mean * sums[2:3]) / D
            coef = jnp.concatenate([mean, rstd, mean_one, mean_two, jnp.zeros((4, T), F32)], axis=0)
            mean, rstd, mean_one, mean_two = [dot_exact(coef, (pick == i).astype(F32), TN) for i in range(4)]
            normed = (mixed[b] - mean) * rstd
            dnorm = og[b].astype(F32) * gate[b].astype(F32) * gain
            dbuf[b] = (rstd * (dnorm - mean_one - normed * mean_two)).astype(BF16)
            d_pass(b)
            back[0, b] = normed.astype(BF16)
        for b in range(2):
            send_back(0, b)

    def back_wait(i):
        for k in range(2):
            dst = finals[i].at[:, pl.ds(k * HD, HD)]
            remote(back.at[i, k], dst, back_s.at[i, k], back_r.at[i, k], partner).wait_recv()

    writes = [pltpu.make_async_copy(placed.at[i], ref, own.at[i]) for i, ref in ((3, out_ref), (4, dgate_ref))]

    def gated():
        back_wait(0)
        for cp in owns:
            cp.wait()
        normed = placed[0].astype(F32)
        gain = gains[0, 0:1, :]
        placed[3] = (normed * gain * placed[1].astype(F32)).astype(BF16)
        placed[4] = (placed[2].astype(F32) * normed * gain).astype(BF16)
        for cp in writes:
            cp.start()

    def finish_keys(b):
        back[3, b] = dvacc[b].astype(BF16)
        send_back(3, b)
        back[2, b] = (dkacc[b] * SCALE).astype(BF16)
        send_back(2, b)

    sums_along()
    keys_before(1, 0)
    keys_before(0, 1)
    sums_across()
    slot_wait(qbuf, q_s, q_r, 2)
    q_pass(2)
    keys_before(0, 2)
    keys_before(1, 1)
    slot_wait(qbuf, q_s, q_r, 3)
    keys_before(0, 3)
    keys_before(1, 2)
    slot_wait(qbuf, q_s, q_r, 4)
    keys_before(1, 3)
    norm()
    keys_after(0, 0)
    keys_after(1, 0)
    keys_after(0, 1)
    query_grad(0)
    send_back(1, 0)
    slot_wait(dbuf, d_s, d_r, 2)
    d_pass(2)
    keys_after(0, 2)
    keys_after(1, 1)
    slot_wait(dbuf, d_s, d_r, 3)
    keys_after(0, 3)
    finish_keys(0)
    query_grad(1)
    send_back(1, 1)
    keys_after(1, 2)
    gated()
    slot_wait(dbuf, d_s, d_r, 4)
    keys_after(1, 3)
    finish_keys(1)

    for e in range(1, 4):
        st(e).wait_send()
    st_across.wait_send()
    gain_copy.wait_send()
    done = lambda cp: cp.wait_send()
    for a in range(2):
        pass_on(kv_routes, (kbuf, vbuf)[a], kv_s.at[a], kv_r.at[a], range(5), done)
    pass_on(q_routes, qbuf, q_s, q_r, range(5), done)
    pass_on(q_routes, dbuf, d_s, d_r, range(5), done)
    for i in range(5):
        for k in range(2):
            home(i, k, done)
            if i < 4:
                back_copy(i, k, done)
    for i in (1, 2, 3):
        back_wait(i)
    for cp in writes:
        cp.wait()


def write_out(*refs):
    src, dst, buf, into, out = refs[:5], refs[5:10], *refs[10:]
    reads = [pltpu.make_async_copy(src[i], buf.at[i], into.at[i]) for i in range(5)]
    writes = [pltpu.make_async_copy(buf.at[i], dst[i], out.at[i]) for i in range(5)]
    for cp in reads:
        cp.start()
    for read, write in zip(reads, writes):
        read.wait()
        write.start()
    for cp in writes:
        cp.wait()


def per_device(queries, key_rows, value_rows, gating, gain_vector, out_grad, user_lengths, cand_counts):
    feat = queries.shape[1]
    block = jax.ShapeDtypeStruct((T, feat), BF16)
    vmem = pl.BlockSpec(memory_space=pltpu.VMEM)
    smem = pl.BlockSpec(memory_space=pltpu.SMEM)
    hbm = pl.BlockSpec(memory_space=pltpu.HBM)
    sem = pltpu.SemaphoreType.DMA
    results = pl.pallas_call(
        kernel,
        out_shape=[block] * 5,
        in_specs=[smem, smem, vmem, hbm, hbm, hbm, hbm, hbm],
        out_specs=[hbm] * 5,
        scratch_shapes=[
            pltpu.VMEM((5, T, HD), BF16),
            pltpu.VMEM((5, T, HD), BF16),
            pltpu.VMEM((5, T, HD), BF16),
            pltpu.VMEM((5, T, HD), BF16),
            pltpu.VMEM((2, T, HD), BF16),
            pltpu.VMEM((2, T, HD), BF16),
            pltpu.VMEM((2, T, HD), F32),
            pltpu.VMEM((2, T, HD), F32),
            pltpu.VMEM((2, T, HD), F32),
            pltpu.VMEM((4, 2, T, HD), BF16),
            pltpu.VMEM((5, T, feat), BF16),
            pltpu.VMEM((2, T, 4 * T), F32),
            pltpu.VMEM((2, T, 4 * T), BF16),
            pltpu.VMEM((2, T, 4 * T), F32),
            pltpu.VMEM((2, T, HD), jnp.int32),
            pltpu.VMEM((2, T, HD), jnp.int32),
            pltpu.VMEM((5, 8, T), jnp.int32),
            pltpu.VMEM((5, 8, T), jnp.int32),
            pltpu.VMEM((6, 8, T), F32),
            pltpu.VMEM((2, 8, 2 * HD), F32),
            sem((5, 2)), sem((5, 2)),
            sem((2, 3)), sem((2, 3)),
            sem((4,)), sem((5,)),
            sem((4,)), sem((5,)),
            sem((4,)), sem((4,)),
            sem, sem,
            sem((4, 2)), sem((4, 2)),
            sem((5,)),
        ],
        compiler_params=pltpu.CompilerParams(
            collective_id=0, has_side_effects=True, vmem_limit_bytes=61 << 20
        ),
        name="hstu",
    )(user_lengths, cand_counts, gain_vector, queries, key_rows, value_rows, gating, out_grad)
    return pl.pallas_call(
        write_out,
        out_shape=[block] * 5,
        in_specs=[hbm] * 5,
        out_specs=[hbm] * 5,
        scratch_shapes=[pltpu.VMEM((5, T, feat), BF16), sem((5,)), sem((5,))],
        name="write_out",
    )(*results)


def solution(mesh):
    tokens = P("ctx", "head")
    return jax.shard_map(
        per_device,
        mesh=mesh,
        in_specs=(tokens, tokens, tokens, tokens, P("head"), tokens, P(), P()),
        out_specs=(tokens,) * 5,
        check_vma=False,
    )
```
